32 devices in a mesh: mem: 4 (over z), sp: 8 (over y, x, core).
Axes of the slice: x: 2, y: 2, z: 4, core: 2. Of those that a mesh axis runs over, the one named last changes fastest.
Arguments:
- span_input: bfloat16 [4, 1024, 5120], P('mem', 'sp'), may hold values from -6 to 6
- w_query: bfloat16 [5120, 4096], P(None, 'sp')
- w_key: bfloat16 [5120, 4096], P(None, 'sp')
- w_value: bfloat16 [5120, 4096], P(None, 'sp'), may hold values from -0.078125 to 0.078125
- memory_kv: bfloat16 [32, 2, 256, 4096], P(('mem', 'sp')), may hold values from -6 to 6
- selected: int32 [4, 8], replicated, may hold values from 0 to 31, as said below
- frame_slot: int32 [32], replicated, may hold values from 0 to 31, as said below
- write_slot: int32 [4, 2], replicated, may hold values from 0 to 31, as said below
Outputs:
- attended: bfloat16 [4, 1024, 4096], P('mem', None, 'sp')
- new_memory: bfloat16 [32, 2, 256, 4096], P(('mem', 'sp'))
The draws below stay inside these ranges and needn't reach their ends.
Inputs may be any that keep to these rules, and one draw needn't show every extreme that they name: `selected`: each row names 8 different frame ids. Of one row's frames, at most 2 have their slot in one block of 8 consecutive slots, and in every row some block holds exactly 2 of them. `frame_slot`: every slot appears exactly once. `write_slot`: all entries differ; the 2 slots of one row lie in different blocks of 8 consecutive slots, and every such block holds exactly 2 entries.
All inputs are finite; a program needn't handle non-finite values.
Results may differ from the reference program's by a relative error of at most 0.0085.
Values may be sent and summed in bfloat16 or wider, within the bound.
A program may use at most 128 MiB of HBM per device.

```python
import jax
import jax.numpy as jnp
from jax import lax

D = 5120
HEADS = 32
HD = 128
MTOK = 256
FRAMES_SPAN = 2
SEL = 8
CAP = 2
SPAN = 1024
POOL = 2
HH = 4096
SLOTS = 32
N_MEM = 4


def projection_pair(key):
    query_part = jax.random.normal(jax.random.fold_in(key, 401), (D, HH), jnp.float32) * D ** (-0.5)
    key_part = jax.random.normal(jax.random.fold_in(key, 402), (D, HH), jnp.float32) * D ** (-0.5)
    return (query_part, key_part)


def draw_w_query(key, part):
    return projection_pair(key)[0].astype(jnp.bfloat16)


def draw_w_key(key, part):
    return projection_pair(key)[1].astype(jnp.bfloat16)


def slot_table(key):
    return jax.random.permutation(jax.random.fold_in(key, 101), SLOTS).astype(jnp.int32)


def draw_frame_slot(key, part):
    return slot_table(key)


def draw_selected(key, part):
    table = slot_table(key)
    inverse = jnp.zeros((SLOTS,), jnp.int32).at[table].set(jnp.arange(SLOTS, dtype=jnp.int32))
    row_width = SLOTS // N_MEM
    inner = jax.random.fold_in(key, 202)
    item_total = N_MEM * CAP
    item_row = jnp.arange(item_total, dtype=jnp.int32) // CAP
    item_copy = jnp.arange(item_total, dtype=jnp.int32) % CAP

    def one_group(group_id):
        group_key = jax.random.fold_in(inner, group_id)
        hot_row = jax.random.randint(jax.random.fold_in(group_key, 1), (), 0, N_MEM)
        order = jax.random.permutation(jax.random.fold_in(group_key, 2), item_total).astype(jnp.int32)
        score = order + (item_row == hot_row).astype(jnp.int32) * item_total
        chosen_items = jnp.argsort(-score, stable=True)[:SEL]
        rows_chosen = item_row[chosen_items]
        copies_chosen = item_copy[chosen_items]
        column_key = jax.random.fold_in(group_key, 3)
        column_perm = jax.vmap(lambda row_id: jax.random.permutation(jax.random.fold_in(column_key, row_id), row_width))(jnp.arange(N_MEM, dtype=jnp.int32))
        columns = column_perm[rows_chosen, copies_chosen]
        return inverse[rows_chosen * row_width + columns]
    return jax.vmap(one_group)(jnp.arange(N_MEM, dtype=jnp.int32)).astype(jnp.int32)


def draw_write_slot(key, part):
    inner = jax.random.fold_in(key, 303)
    row_width = SLOTS // N_MEM
    row_order = jax.random.permutation(jax.random.fold_in(inner, 1), N_MEM).astype(jnp.int32)
    column_key = jax.random.fold_in(inner, 2)
    column_perm = jax.vmap(lambda row_id: jax.random.permutation(jax.random.fold_in(column_key, row_id), row_width))(jnp.arange(N_MEM, dtype=jnp.int32))
    entries = []
    for frame_id in range(FRAMES_SPAN):
        rows_here = jnp.roll(row_order, -frame_id)
        entries.append(rows_here * row_width + column_perm[rows_here, frame_id])
    return jnp.stack(entries, axis=1).astype(jnp.int32)


def steps_of(stream_key, dims, pieces, low, top_value):
    def one(axis_at, shards_of):
        draws = jax.random.uniform(jax.random.fold_in(jax.random.fold_in(stream_key, 6), axis_at), (shards_of,), jnp.float32, low / len(pieces), top_value / len(pieces))
        return jnp.repeat(jnp.exp(draws), dims[axis_at] // shards_of).reshape((-1,) + (1,) * (len(dims) - axis_at - 1))

    loudness = one(*pieces[0])
    for cut in pieces[1:]:
        loudness = loudness * one(*cut)
    return loudness


def scatter_about(stream_key, extent, scale, limit, cuts=(), kind=jnp.bfloat16):
    factor_of = steps_of(stream_key, extent, cuts, -0.22, 0.18) if cuts else 1.0
    values = jax.random.normal(stream_key, extent, jnp.float32) * scale * factor_of
    return jnp.minimum(jnp.maximum(values, -limit), limit).astype(kind)


def setup_inputs(seed: int = 0) -> dict:
    arg_keys = jax.random.split(jax.random.key(seed), 9)
    return {
        "span_input": scatter_about(arg_keys[0], (N_MEM, SPAN, D), 1.0, 6.0, ((0, 4), (1, 8))),
        "w_query": draw_w_query(jax.random.fold_in(arg_keys[8], 71), 0),
        "w_key": draw_w_key(jax.random.fold_in(arg_keys[8], 71), 0),
        "w_value": scatter_about(arg_keys[3], (D, HH), D ** -0.5, 0.078125, ((1, 8),)),
        "memory_kv": scatter_about(arg_keys[4], (SLOTS, 2, MTOK, HH), 1.0, 6.0, ((0, 32),)),
        "selected": draw_selected(jax.random.fold_in(arg_keys[8], 71), 0),
        "frame_slot": draw_frame_slot(jax.random.fold_in(arg_keys[8], 71), 0),
        "write_slot": draw_write_slot(jax.random.fold_in(arg_keys[8], 71), 0),
    }


def attend(query, keys, values, bias):
    count_q = query.shape[0]
    block_rows = min(512, count_q)
    blocks = query.reshape(count_q // block_rows, block_rows, query.shape[1])
    scale_factor = HD ** -0.5

    def one_block(query_block):
        scores = lax.dot_general(query_block, keys, (((1,), (1,)), ((), ())), preferred_element_type=jnp.float32)
        scores = scores * scale_factor + bias[None, :]
        peak = jnp.max(scores, axis=1, keepdims=True)
        weights = jnp.exp(scores - peak)
        totals = jnp.sum(weights, axis=1, keepdims=True)
        mixed = jnp.dot(weights.astype(jnp.bfloat16), values, preferred_element_type=jnp.float32)
        return (mixed / totals).astype(jnp.bfloat16)

    return lax.map(one_block, blocks).reshape(count_q, query.shape[1])


def reference(span_input, w_query, w_key, w_value, memory_kv, selected, frame_slot, write_slot):
    def one_group(group_args):
        rows_in, chosen = group_args
        query = jnp.dot(rows_in, w_query, preferred_element_type=jnp.float32).astype(jnp.bfloat16)
        key_self = jnp.dot(rows_in, w_key, preferred_element_type=jnp.float32).astype(jnp.bfloat16)
        value_self = jnp.dot(rows_in, w_value, preferred_element_type=jnp.float32).astype(jnp.bfloat16)
        slot_ids = jnp.take(frame_slot, chosen, axis=0).astype(jnp.int32)
        frames = jnp.take(memory_kv, slot_ids, axis=0)
        keys_all = jnp.concatenate([key_self, frames[:, 0].reshape(SEL * MTOK, HH)], axis=0)
        values_all = jnp.concatenate([value_self, frames[:, 1].reshape(SEL * MTOK, HH)], axis=0)
        bias = jnp.zeros((SPAN + SEL * MTOK,), jnp.float32)
        heads_query = query.reshape(SPAN, HEADS, HD).transpose(1, 0, 2)
        heads_key = keys_all.reshape(-1, HEADS, HD).transpose(1, 0, 2)
        heads_value = values_all.reshape(-1, HEADS, HD).transpose(1, 0, 2)
        outputs = lax.map(lambda triple: attend(triple[0], triple[1], triple[2], bias),
                          (heads_query, heads_key, heads_value))
        outputs = outputs.transpose(1, 0, 2).reshape(SPAN, HH)
        pooled_key = jnp.mean(key_self.astype(jnp.float32).reshape(FRAMES_SPAN, MTOK, POOL, HH), axis=2)
        pooled_value = jnp.mean(value_self.astype(jnp.float32).reshape(FRAMES_SPAN, MTOK, POOL, HH), axis=2)
        pooled = jnp.stack([pooled_key, pooled_value], axis=1).astype(jnp.bfloat16)
        return outputs, pooled

    attended, pooled = lax.map(one_group, (span_input, selected))
    flat_slots = write_slot.reshape(N_MEM * FRAMES_SPAN).astype(jnp.int32)
    new_memory = memory_kv.at[flat_slots].set(pooled.reshape(N_MEM * FRAMES_SPAN, 2, MTOK, HH))
    return attended, new_memory
```

```python
import functools
import math

import jax
import jax.numpy as jnp
from jax import lax
from jax.experimental import pallas as pl
from jax.experimental.pallas import tpu as pltpu
from jax.sharding import PartitionSpec as P

HD = 128
MTOK = 256
FRAMES_SPAN = 2
CAP = 2
SEL = 8
HALVES = 2
CHUNKS = 2 * HALVES
TOK = MTOK // HALVES
NEG_FILL = -1e30
MESH = pl.DeviceIdType.MESH
VMEM_LIMIT = 58 * 1024 * 1024


def greet(groups, width, g, c):
    barrier = pltpu.get_barrier_semaphore()
    for o in range(1, width):
        pl.semaphore_signal(
            barrier, inc=1, device_id=(g, lax.rem(c + o, width)), device_id_type=MESH
        )
    for o in range(1, groups):
        pl.semaphore_signal(
            barrier, inc=1, device_id=(lax.rem(g + o, groups), c), device_id_type=MESH
        )
    pl.semaphore_wait(barrier, width + groups - 2)


def project_kernel(groups, width, pool, pick, x, wq, wk, wv, mem, qkv, pooled, got, *scratch):
    rows = scratch[:CHUNKS]
    (sendbuf, xg, w3, w_sem, own_sem, mem_send, mem_recv, x_send, x_recv, f_send, f_recv,
     z_send, z_recv, z_own) = scratch[CHUNKS:]
    g = lax.axis_index("mem")
    c = lax.axis_index("sp")
    cols = wq.shape[1]
    block = x.shape[0]
    pairs = width // 2
    me_pair = c // 2
    lane = lax.rem(c, 2)
    sibling = me_pair * 2 + 1 - lane
    lane_rows = pl.ds(pl.multiple_of(lane * block, block), block)
    greet(groups, width, g, c)

    own = []
    sends = []

    def mem_copy(ch, o):
        to = lax.rem(c + o, width)
        return pltpu.make_async_remote_copy(
            src_ref=mem.at[pl.ds(ch * TOK, TOK), pl.ds(pl.multiple_of(to * cols, cols), cols)],
            dst_ref=rows[ch].at[c],
            send_sem=mem_send.at[ch, o],
            recv_sem=mem_recv.at[ch, o],
            device_id=(g, to),
            device_id_type=MESH,
        )

    def x_copy(j):
        to = sibling if j == 0 else lax.rem(c + 2 * j, width)
        return pltpu.make_async_remote_copy(
            src_ref=x,
            dst_ref=xg.at[me_pair, lane_rows],
            send_sem=x_send.at[j],
            recv_sem=x_recv.at[j],
            device_id=(g, to),
            device_id_type=MESH,
        )

    def send_mem(ch):
        copy = pltpu.make_async_copy(
            mem.at[pl.ds(ch * TOK, TOK), pl.ds(pl.multiple_of(c * cols, cols), cols)],
            rows[ch].at[c],
            own_sem.at[ch],
        )
        copy.start()
        own.append(copy)
        for o in range(1, width):
            copy = mem_copy(ch, o)
            copy.start()
            sends.append(copy)

    def send_x(j):
        copy = x_copy(j)
        copy.start()
        sends.append(copy)

    own_x = pltpu.make_async_copy(x, xg.at[me_pair, lane_rows], own_sem.at[CHUNKS])
    w_copies = [
        pltpu.make_async_copy(w, w3.at[i], w_sem.at[i]) for i, w in enumerate((wq, wk, wv))
    ]
    send_mem(0)
    send_x(0)
    own_x.start()
    for copy in w_copies:
        copy.start()
    for step in range(1, max(CHUNKS, pairs)):
        if step < CHUNKS:
            send_mem(step)
        if step < pairs:
            send_x(step)

    z_copies = []
    z_local = []

    def fetch(ch):
        own[ch].wait()
        for o in range(1, width):
            mem_copy(ch, o).wait_recv()
        for o in list(range(1, groups)) + [0]:
            to = lax.rem(g + o, groups)
            for r in range(CAP):
                sendbuf[ch, to, r] = rows[ch][pick[to * CAP + r]]
            if o == 0:
                copy = pltpu.make_async_copy(sendbuf.at[ch, g], got.at[ch, g], z_own.at[ch])
                z_local.append(copy)
            else:
                copy = pltpu.make_async_remote_copy(
                    src_ref=sendbuf.at[ch, to],
                    dst_ref=got.at[ch, g],
                    send_sem=z_send.at[ch, o],
                    recv_sem=z_recv.at[ch, o],
                    device_id=(to, c),
                    device_id_type=MESH,
                )
                z_copies.append(copy)
            copy.start()

    small = 2 * block // pool
    row_id = lax.broadcasted_iota(jnp.int32, (small, 2 * block), 0) * pool
    col_id = lax.broadcasted_iota(jnp.int32, (small, 2 * block), 1)
    inside = (col_id >= row_id) & (col_id < row_id + pool)
    averager = jnp.where(inside, 1.0 / pool, 0.0).astype(jnp.bfloat16)
    forwards = []

    def project(j):
        pair = lax.rem(me_pair - j + pairs, pairs)
        x_copy(j).wait_recv()
        if j == 0:
            own_x.wait()
            for copy in w_copies:
                copy.wait()
        else:
            copy = pltpu.make_async_remote_copy(
                src_ref=xg.at[pair, lane_rows],
                dst_ref=xg.at[pair, lane_rows],
                send_sem=f_send.at[j],
                recv_sem=f_recv.at[j],
                device_id=(g, sibling),
                device_id_type=MESH,
            )
            copy.start()
            forwards.append(copy)
            copy.wait_recv()
        out_rows = pl.ds(pl.multiple_of(pair * 2 * block, 2 * block), 2 * block)

        def one(i, carry):
            part = jnp.dot(xg[pair], w3[i], preferred_element_type=jnp.float32)
            qkv[i, out_rows, :] = part.astype(jnp.bfloat16)
            return carry

        lax.fori_loop(0, 3, one, 0)
        small_rows = pl.ds(pl.multiple_of(pair * small, small), small)
        for i in range(2):
            mean = jnp.dot(averager, qkv[i + 1, out_rows, :], preferred_element_type=jnp.float32)
            pooled[i, small_rows, :] = mean.astype(jnp.bfloat16)

    for step in range(max(CHUNKS, pairs)):
        if step < CHUNKS:
            fetch(step)
        if step < pairs:
            project(step)

    for copy in sends + forwards:
        copy.wait_send()
    for copy in z_local:
        copy.wait()
    for copy in z_copies:
        copy.wait()


def attend_kernel(groups, width, wsel, rsel, bias, qkv, got, pooled, att, assembled, *scratch):
    arrived = scratch[:CHUNKS]
    wbuf, rbuf, z_send, z_recv, r_send, r_recv, r_own = scratch[CHUNKS:]
    g = lax.axis_index("mem")
    c = lax.axis_index("sp")
    span, cols = att.shape
    heads = cols // HD
    half = got.shape[0] // 2
    greet(groups, width, g, c)
    z_copies = []
    for ch in range(CHUNKS):
        for o in list(range(1, groups)) + [0]:
            to = lax.rem(g + o, groups)
            piece = pooled[ch // HALVES, wsel[to], ch % HALVES]
            if o == 0:
                arrived[ch][g] = piece
                continue
            wbuf[ch, to] = piece
            copy = pltpu.make_async_remote_copy(
                src_ref=wbuf.at[ch, to],
                dst_ref=arrived[ch].at[g],
                send_sem=z_send.at[ch, o],
                recv_sem=z_recv.at[ch, o],
                device_id=(to, c),
                device_id_type=MESH,
            )
            copy.start()
            z_copies.append((ch, copy))

    r_copies = []
    r_local = []

    def regroup(ch):
        for at, copy in z_copies:
            if at == ch:
                copy.wait_recv()
        for o in list(range(1, width)) + [0]:
            to = lax.rem(c + o, width)
            rbuf[ch, to] = arrived[ch][rsel[to]]
            place = assembled.at[
                pl.ds(ch * TOK, TOK), pl.ds(pl.multiple_of(c * cols, cols), cols)
            ]
            if o == 0:
                copy = pltpu.make_async_copy(rbuf.at[ch, to], place, r_own.at[ch])
                r_local.append(copy)
            else:
                copy = pltpu.make_async_remote_copy(
                    src_ref=rbuf.at[ch, to],
                    dst_ref=place,
                    send_sem=r_send.at[ch, o],
                    recv_sem=r_recv.at[ch, o],
                    device_id=(g, to),
                    device_id_type=MESH,
                )
                r_copies.append(copy)
            copy.start()

    factor = HD ** (-0.5) * math.log2(math.e)
    block = min(256, span)
    nt = (((1,), (1,)), ((), ()))

    def attend(h):
        lanes = slice(h * HD, (h + 1) * HD)

        def one(i, carry):
            rows = pl.ds(pl.multiple_of(i * block, block), block)
            query = qkv[0, rows, lanes]
            own = lax.dot_general(query, qkv[1, :, lanes], nt, preferred_element_type=jnp.float32)
            far = lax.dot_general(
                query, got[0:half, lanes], nt, preferred_element_type=jnp.float32
            )
            if bias is not None:
                far = far + bias[...]
            peak = jnp.maximum(
                jnp.max(own, axis=1, keepdims=True), jnp.max(far, axis=1, keepdims=True)
            )
            own = jnp.exp2((own - peak) * factor)
            far = jnp.exp2((far - peak) * factor)
            totals = jnp.sum(own, axis=1, keepdims=True) + jnp.sum(far, axis=1, keepdims=True)
            mixed = jnp.dot(
                own.astype(jnp.bfloat16), qkv[2, :, lanes], preferred_element_type=jnp.float32
            )
            mixed += jnp.dot(
                far.astype(jnp.bfloat16),
                got[half : 2 * half, lanes],
                preferred_element_type=jnp.float32,
            )
            att[rows, lanes] = (mixed / totals).astype(jnp.bfloat16)
            return carry

        lax.fori_loop(0, span // block, one, 0)

    for step in range(max(heads, CHUNKS)):
        if step < heads:
            attend(step)
        if step < CHUNKS:
            regroup(step)
    for _, copy in z_copies:
        copy.wait_send()
    for copy in r_local:
        copy.wait()
    for copy in r_copies:
        copy.wait()


def local(span_input, w_query, w_key, w_value, memory_kv, selected, frame_slot, write_slot):
    groups = lax.axis_size("mem")
    width = lax.axis_size("sp")
    g = lax.axis_index("mem")
    c = lax.axis_index("sp")
    depth, cols = w_query.shape
    block = span_input.shape[1]
    span = block * width
    pairs = width // 2
    pool = span // (FRAMES_SPAN * MTOK)
    features = memory_kv.shape[3]

    slot_ids = jnp.take(frame_slot, selected, axis=0)
    slot_row = slot_ids // width
    in_row = slot_row == g
    rank = jnp.cumsum(in_row.astype(jnp.int32), axis=1) - 1
    hit = in_row[:, None, :] & (rank[:, None, :] == jnp.arange(CAP, dtype=jnp.int32)[None, :, None])
    pick = jnp.sum(jnp.where(hit, (slot_ids % width)[:, None, :], 0), axis=2).reshape(-1)

    vmem = pl.BlockSpec(memory_space=pltpu.VMEM)
    smem = pl.BlockSpec(memory_space=pltpu.SMEM)
    anywhere = pl.BlockSpec(memory_space=pl.ANY)
    bf16 = jnp.bfloat16
    dma = pltpu.SemaphoreType.DMA
    qkv, pooled, got = pl.pallas_call(
        functools.partial(project_kernel, groups, width, pool),
        out_shape=(
            jax.ShapeDtypeStruct((3, span, cols), bf16),
            jax.ShapeDtypeStruct((2, FRAMES_SPAN * MTOK, cols), bf16),
            jax.ShapeDtypeStruct((CHUNKS, groups, CAP, TOK, cols), bf16),
        ),
        in_specs=[smem] + [anywhere] * 5,
        out_specs=(vmem, vmem, anywhere),
        scratch_shapes=[pltpu.VMEM((width, TOK, cols), bf16)] * CHUNKS
        + [
            pltpu.VMEM((CHUNKS, groups, CAP, TOK, cols), bf16),
            pltpu.VMEM((pairs, 2 * block, depth), bf16),
            pltpu.VMEM((3, depth, cols), bf16),
            dma((3,)),
            dma((CHUNKS + 1,)),
            dma((CHUNKS, width)),
            dma((CHUNKS, width)),
            dma((pairs,)),
            dma((pairs,)),
            dma((pairs,)),
            dma((pairs,)),
            dma((CHUNKS, groups)),
            dma((CHUNKS, groups)),
            dma((CHUNKS,)),
        ],
        compiler_params=pltpu.CompilerParams(
            collective_id=0, has_side_effects=True, vmem_limit_bytes=VMEM_LIMIT
        ),
        name="project_and_fetch",
    )(pick, span_input[0], w_query, w_key, w_value, memory_kv.reshape(2 * MTOK, features))

    own_slots = lax.dynamic_index_in_dim(write_slot, g, 0, keepdims=False)
    rows_m = jnp.arange(groups, dtype=jnp.int32)
    frames = jnp.arange(FRAMES_SPAN, dtype=jnp.int32)
    wsel = jnp.sum(
        jnp.where((own_slots // width)[None, :] == rows_m[:, None], frames[None, :], 0), axis=1
    )
    targets = g * width + jnp.arange(width, dtype=jnp.int32)
    match = jnp.any(write_slot[None, :, :] == targets[:, None, None], axis=2)
    rsel = jnp.sum(jnp.where(match, rows_m[None, :], 0), axis=1)

    operands = [wsel, rsel]
    specs = [smem, smem]
    kernel = functools.partial(attend_kernel, groups, width)
    if groups * CAP != SEL:
        own_rows = lax.dynamic_index_in_dim(slot_row, g, 0, keepdims=False)
        counts = jnp.sum((own_rows[None, :] == rows_m[:, None]).astype(jnp.int32), axis=1)
        live = jnp.arange(CAP, dtype=jnp.int32)[None, :] < counts[:, None]
        fill = jnp.where(live, 0.0, NEG_FILL).astype(jnp.float32)
        fill = jnp.broadcast_to(fill[None, :, :, None], (HALVES, groups, CAP, TOK))
        operands.append(fill.reshape(1, -1))
        specs.append(vmem)
    else:
        kernel = functools.partial(without_bias, kernel)
    attended, assembled = pl.pallas_call(
        kernel,
        out_shape=(
            jax.ShapeDtypeStruct((span, cols), bf16),
            jax.ShapeDtypeStruct((2 * MTOK, features), bf16),
        ),
        in_specs=specs + [vmem] * 3,
        out_specs=(vmem, anywhere),
        scratch_shapes=[pltpu.VMEM((groups, TOK, cols), bf16)] * CHUNKS
        + [
            pltpu.VMEM((CHUNKS, groups, TOK, cols), bf16),
            pltpu.VMEM((CHUNKS, width, TOK, cols), bf16),
            dma((CHUNKS, groups)),
            dma((CHUNKS, groups)),
            dma((CHUNKS, width)),
            dma((CHUNKS, width)),
            dma((CHUNKS,)),
        ],
        compiler_params=pltpu.CompilerParams(
            collective_id=1, has_side_effects=True, vmem_limit_bytes=VMEM_LIMIT
        ),
        name="attend_and_write",
    )(
        *operands,
        qkv,
        got.reshape(-1, cols),
        pooled.reshape(2, FRAMES_SPAN, HALVES, TOK, cols),
    )
    written = jnp.any(write_slot == g * width + c)
    new_memory = jnp.where(written, assembled.reshape(memory_kv.shape), memory_kv)
    return (attended[None], new_memory)


def without_bias(kernel, wsel, rsel, *rest):
    kernel(wsel, rsel, None, *rest)


def solution(mesh):
    placed = (
        P("mem", "sp", None),
        P(None, "sp"),
        P(None, "sp"),
        P(None, "sp"),
        P(("mem", "sp"), None, None, None),
        P(),
        P(),
        P(),
    )
    return jax.shard_map(
        local,
        mesh=mesh,
        in_specs=placed,
        out_specs=(P("mem", None, "sp"), P(("mem", "sp"), None, None, None)),
        check_vma=False,
    )
```

```python
import functools
import math

import jax
import jax.numpy as jnp
from jax import lax
from jax.experimental import pallas as pl
from jax.experimental.pallas import tpu as pltpu
from jax.sharding import PartitionSpec as P

HD = 128
MTOK = 256
FRAMES_SPAN = 2
CAP = 2
SEL = 8
HALVES = 2
CHUNKS = 2 * HALVES
TOK = MTOK // HALVES
NEG_FILL = -1e30
MESH = pl.DeviceIdType.MESH
VMEM_LIMIT = 58 * 1024 * 1024


def greet(groups, width, g, c):
    barrier = pltpu.get_barrier_semaphore()
    for o in range(1, width):
        pl.semaphore_signal(
            barrier, inc=1, device_id=(g, lax.rem(c + o, width)), device_id_type=MESH
        )
    for o in range(1, groups):
        pl.semaphore_signal(
            barrier, inc=1, device_id=(lax.rem(g + o, groups), c), device_id_type=MESH
        )
    pl.semaphore_wait(barrier, width + groups - 2)


def project_kernel(groups, width, pool, pick, x, wq, wk, wv, mem, qkv, pooled, got, *scratch):
    rows = scratch[:CHUNKS]
    (sendbuf, xg, w3, w_sem, own_sem, mem_send, mem_recv, x_send, x_recv, f_send, f_recv,
     z_send, z_recv, z_own) = scratch[CHUNKS:]
    g = lax.axis_index("mem")
    c = lax.axis_index("sp")
    cols = wq.shape[1]
    block = x.shape[0]
    pairs = width // 2
    me_pair = c // 2
    lane = lax.rem(c, 2)
    sibling = me_pair * 2 + 1 - lane
    lane_rows = pl.ds(pl.multiple_of(lane * block, block), block)
    greet(groups, width, g, c)

    own = []
    sends = []

    def mem_copy(ch, o):
        to = lax.rem(c + o, width)
        return pltpu.make_async_remote_copy(
            src_ref=mem.at[pl.ds(ch * TOK, TOK), pl.ds(pl.multiple_of(to * cols, cols), cols)],
            dst_ref=rows[ch].at[c],
            send_sem=mem_send.at[ch, o],
            recv_sem=mem_recv.at[ch, o],
            device_id=(g, to),
            device_id_type=MESH,
        )

    def x_copy(j):
        to = sibling if j == 0 else lax.rem(c + 2 * j, width)
        return pltpu.make_async_remote_copy(
            src_ref=x,
            dst_ref=xg.at[me_pair, lane_rows],
            send_sem=x_send.at[j],
            recv_sem=x_recv.at[j],
            device_id=(g, to),
            device_id_type=MESH,
        )

    def send_mem(ch):
        copy = pltpu.make_async_copy(
            mem.at[pl.ds(ch * TOK, TOK), pl.ds(pl.multiple_of(c * cols, cols), cols)],
            rows[ch].at[c],
            own_sem.at[ch],
        )
        copy.start()
        own.append(copy)
        for o in range(1, width):
            copy = mem_copy(ch, o)
            copy.start()
            sends.append(copy)

    def send_x(j):
        copy = x_copy(j)
        copy.start()
        sends.append(copy)

    own_x = pltpu.make_async_copy(x, xg.at[me_pair, lane_rows], own_sem.at[CHUNKS])
    w_copies = [
        pltpu.make_async_copy(w, w3.at[i], w_sem.at[i]) for i, w in enumerate((wq, wk, wv))
    ]
    send_mem(0)
    send_x(0)
    own_x.start()
    for copy in w_copies:
        copy.start()

    z_copies = []
    z_local = []

    def fetch(ch):
        own[ch].wait()
        for o in range(1, width):
            mem_copy(ch, o).wait_recv()
        for o in list(range(1, groups)) + [0]:
            to = lax.rem(g + o, groups)
            for r in range(CAP):
                sendbuf[ch, to, r] = rows[ch][pick[to * CAP + r]]
            if o == 0:
                copy = pltpu.make_async_copy(sendbuf.at[ch, g], got.at[ch, g], z_own.at[ch])
                z_local.append(copy)
            else:
                copy = pltpu.make_async_remote_copy(
                    src_ref=sendbuf.at[ch, to],
                    dst_ref=got.at[ch, g],
                    send_sem=z_send.at[ch, o],
                    recv_sem=z_recv.at[ch, o],
                    device_id=(to, c),
                    device_id_type=MESH,
                )
                z_copies.append(copy)
            copy.start()

    small = 2 * block // pool
    row_id = lax.broadcasted_iota(jnp.int32, (small, 2 * block), 0) * pool
    col_id = lax.broadcasted_iota(jnp.int32, (small, 2 * block), 1)
    inside = (col_id >= row_id) & (col_id < row_id + pool)
    averager = jnp.where(inside, 1.0 / pool, 0.0).astype(jnp.bfloat16)
    forwards = []

    def project(j):
        pair = lax.rem(me_pair - j + pairs, pairs)
        x_copy(j).wait_recv()
        if j == 0:
            own_x.wait()
            for copy in w_copies:
                copy.wait()
        else:
            copy = pltpu.make_async_remote_copy(
                src_ref=xg.at[pair, lane_rows],
                dst_ref=xg.at[pair, lane_rows],
                send_sem=f_send.at[j],
                recv_sem=f_recv.at[j],
                device_id=(g, sibling),
                device_id_type=MESH,
            )
            copy.start()
            forwards.append(copy)
            copy.wait_recv()
        out_rows = pl.ds(pl.multiple_of(pair * 2 * block, 2 * block), 2 * block)

        def one(i, carry):
            part = jnp.dot(xg[pair], w3[i], preferred_element_type=jnp.float32)
            qkv[i, out_rows, :] = part.astype(jnp.bfloat16)
            return carry

        lax.fori_loop(0, 3, one, 0)
        small_rows = pl.ds(pl.multiple_of(pair * small, small), small)
        for i in range(2):
            mean = jnp.dot(averager, qkv[i + 1, out_rows, :], preferred_element_type=jnp.float32)
            pooled[i, small_rows, :] = mean.astype(jnp.bfloat16)

    for step in range(max(CHUNKS, pairs + 1)):
        if step < CHUNKS:
            fetch(step)
        if step + 1 < CHUNKS:
            send_mem(step + 1)
        if 1 <= step < pairs:
            send_x(step)
        if step == 0:
            project(0)
        elif 1 <= step - 1 < pairs:
            project(step - 1)

    for copy in sends + forwards:
        copy.wait_send()
    for copy in z_local:
        copy.wait()
    for copy in z_copies:
        copy.wait()


def attend_kernel(groups, width, wsel, rsel, bias, qkv, got, pooled, att, assembled, *scratch):
    arrived = scratch[:CHUNKS]
    wbuf, rbuf, z_send, z_recv, r_send, r_recv, r_own = scratch[CHUNKS:]
    g = lax.axis_index("mem")
    c = lax.axis_index("sp")
    span, cols = att.shape
    heads = cols // HD
    half = got.shape[0] // 2
    greet(groups, width, g, c)
    z_copies = []

    def send_write(ch):
        for o in list(range(1, groups)) + [0]:
            to = lax.rem(g + o, groups)
            piece = pooled[ch // HALVES, wsel[to], ch % HALVES]
            if o == 0:
                arrived[ch][g] = piece
                continue
            wbuf[ch, to] = piece
            copy = pltpu.make_async_remote_copy(
                src_ref=wbuf.at[ch, to],
                dst_ref=arrived[ch].at[g],
                send_sem=z_send.at[ch, o],
                recv_sem=z_recv.at[ch, o],
                device_id=(to, c),
                device_id_type=MESH,
            )
            copy.start()
            z_copies.append((ch, copy))

    r_copies = []
    r_local = []

    def regroup(ch):
        for at, copy in z_copies:
            if at == ch:
                copy.wait_recv()
        if ch + 2 < CHUNKS:
            send_write(ch + 2)
        for o in list(range(1, width)) + [0]:
            to = lax.rem(c + o, width)
            rbuf[ch, to] = arrived[ch][rsel[to]]
            place = assembled.at[
                pl.ds(ch * TOK, TOK), pl.ds(pl.multiple_of(c * cols, cols), cols)
            ]
            if o == 0:
                copy = pltpu.make_async_copy(rbuf.at[ch, to], place, r_own.at[ch])
                r_local.append(copy)
            else:
                copy = pltpu.make_async_remote_copy(
                    src_ref=rbuf.at[ch, to],
                    dst_ref=place,
                    send_sem=r_send.at[ch, o],
                    recv_sem=r_recv.at[ch, o],
                    device_id=(g, to),
                    device_id_type=MESH,
                )
                r_copies.append(copy)
            copy.start()

    factor = HD ** (-0.5) * math.log2(math.e)
    block = min(256, span)
    nt = (((1,), (1,)), ((), ()))

    def attend(h):
        lanes = slice(h * HD, (h + 1) * HD)

        def one(i, carry):
            rows = pl.ds(pl.multiple_of(i * block, block), block)
            query = qkv[0, rows, lanes]
            own = lax.dot_general(query, qkv[1, :, lanes], nt, preferred_element_type=jnp.float32)
            far = lax.dot_general(
                query, got[0:half, lanes], nt, preferred_element_type=jnp.float32
            )
            if bias is not None:
                far = far + bias[...]
            peak = jnp.maximum(
                jnp.max(own, axis=1, keepdims=True), jnp.max(far, axis=1, keepdims=True)
            )
            own = jnp.exp2((own - peak) * factor)
            far = jnp.exp2((far - peak) * factor)
            totals = jnp.sum(own, axis=1, keepdims=True) + jnp.sum(far, axis=1, keepdims=True)
            mixed = jnp.dot(
                own.astype(jnp.bfloat16), qkv[2, :, lanes], preferred_element_type=jnp.float32
            )
            mixed += jnp.dot(
                far.astype(jnp.bfloat16),
                got[half : 2 * half, lanes],
                preferred_element_type=jnp.float32,
            )
            att[rows, lanes] = (mixed / totals).astype(jnp.bfloat16)
            return carry

        lax.fori_loop(0, span // block, one, 0)

    send_write(0)
    send_write(1)
    for step in range(max(heads, CHUNKS)):
        if step < heads:
            attend(step)
        if step < CHUNKS:
            regroup(step)
    for _, copy in z_copies:
        copy.wait_send()
    for copy in r_local:
        copy.wait()
    for copy in r_copies:
        copy.wait()


def local(span_input, w_query, w_key, w_value, memory_kv, selected, frame_slot, write_slot):
    groups = lax.axis_size("mem")
    width = lax.axis_size("sp")
    g = lax.axis_index("mem")
    c = lax.axis_index("sp")
    depth, cols = w_query.shape
    block = span_input.shape[1]
    span = block * width
    pairs = width // 2
    pool = span // (FRAMES_SPAN * MTOK)
    features = memory_kv.shape[3]

    slot_ids = jnp.take(frame_slot, selected, axis=0)
    slot_row = slot_ids // width
    in_row = slot_row == g
    rank = jnp.cumsum(in_row.astype(jnp.int32), axis=1) - 1
    hit = in_row[:, None, :] & (rank[:, None, :] == jnp.arange(CAP, dtype=jnp.int32)[None, :, None])
    pick = jnp.sum(jnp.where(hit, (slot_ids % width)[:, None, :], 0), axis=2).reshape(-1)

    vmem = pl.BlockSpec(memory_space=pltpu.VMEM)
    smem = pl.BlockSpec(memory_space=pltpu.SMEM)
    anywhere = pl.BlockSpec(memory_space=pl.ANY)
    bf16 = jnp.bfloat16
    dma = pltpu.SemaphoreType.DMA
    qkv, pooled, got = pl.pallas_call(
        functools.partial(project_kernel, groups, width, pool),
        out_shape=(
            jax.ShapeDtypeStruct((3, span, cols), bf16),
            jax.ShapeDtypeStruct((2, FRAMES_SPAN * MTOK, cols), bf16),
            jax.ShapeDtypeStruct((CHUNKS, groups, CAP, TOK, cols), bf16),
        ),
        in_specs=[smem] + [anywhere] * 5,
        out_specs=(vmem, vmem, anywhere),
        scratch_shapes=[pltpu.VMEM((width, TOK, cols), bf16)] * CHUNKS
        + [
            pltpu.VMEM((CHUNKS, groups, CAP, TOK, cols), bf16),
            pltpu.VMEM((pairs, 2 * block, depth), bf16),
            pltpu.VMEM((3, depth, cols), bf16),
            dma((3,)),
            dma((CHUNKS + 1,)),
            dma((CHUNKS, width)),
            dma((CHUNKS, width)),
            dma((pairs,)),
            dma((pairs,)),
            dma((pairs,)),
            dma((pairs,)),
            dma((CHUNKS, groups)),
            dma((CHUNKS, groups)),
            dma((CHUNKS,)),
        ],
        compiler_params=pltpu.CompilerParams(
            collective_id=0, has_side_effects=True, vmem_limit_bytes=VMEM_LIMIT
        ),
        name="project_and_fetch",
    )(pick, span_input[0], w_query, w_key, w_value, memory_kv.reshape(2 * MTOK, features))

    own_slots = lax.dynamic_index_in_dim(write_slot, g, 0, keepdims=False)
    rows_m = jnp.arange(groups, dtype=jnp.int32)
    frames = jnp.arange(FRAMES_SPAN, dtype=jnp.int32)
    wsel = jnp.sum(
        jnp.where((own_slots // width)[None, :] == rows_m[:, None], frames[None, :], 0), axis=1
    )
    targets = g * width + jnp.arange(width, dtype=jnp.int32)
    match = jnp.any(write_slot[None, :, :] == targets[:, None, None], axis=2)
    rsel = jnp.sum(jnp.where(match, rows_m[None, :], 0), axis=1)

    operands = [wsel, rsel]
    specs = [smem, smem]
    kernel = functools.partial(attend_kernel, groups, width)
    if groups * CAP != SEL:
        own_rows = lax.dynamic_index_in_dim(slot_row, g, 0, keepdims=False)
        counts = jnp.sum((own_rows[None, :] == rows_m[:, None]).astype(jnp.int32), axis=1)
        live = jnp.arange(CAP, dtype=jnp.int32)[None, :] < counts[:, None]
        fill = jnp.where(live, 0.0, NEG_FILL).astype(jnp.float32)
        fill = jnp.broadcast_to(fill[None, :, :, None], (HALVES, groups, CAP, TOK))
        operands.append(fill.reshape(1, -1))
        specs.append(vmem)
    else:
        kernel = functools.partial(without_bias, kernel)
    attended, assembled = pl.pallas_call(
        kernel,
        out_shape=(
            jax.ShapeDtypeStruct((span, cols), bf16),
            jax.ShapeDtypeStruct((2 * MTOK, features), bf16),
        ),
        in_specs=specs + [vmem] * 3,
        out_specs=(vmem, anywhere),
        scratch_shapes=[pltpu.VMEM((groups, TOK, cols), bf16)] * CHUNKS
        + [
            pltpu.VMEM((CHUNKS, groups, TOK, cols), bf16),
            pltpu.VMEM((CHUNKS, width, TOK, cols), bf16),
            dma((CHUNKS, groups)),
            dma((CHUNKS, groups)),
            dma((CHUNKS, width)),
            dma((CHUNKS, width)),
            dma((CHUNKS,)),
        ],
        compiler_params=pltpu.CompilerParams(
            collective_id=1, has_side_effects=True, vmem_limit_bytes=VMEM_LIMIT
        ),
        name="attend_and_write",
    )(
        *operands,
        qkv,
        got.reshape(-1, cols),
        pooled.reshape(2, FRAMES_SPAN, HALVES, TOK, cols),
    )
    written = jnp.any(write_slot == g * width + c)
    new_memory = jnp.where(written, assembled.reshape(memory_kv.shape), memory_kv)
    return (attended[None], new_memory)


def without_bias(kernel, wsel, rsel, *rest):
    kernel(wsel, rsel, None, *rest)


def solution(mesh):
    placed = (
        P("mem", "sp", None),
        P(None, "sp"),
        P(None, "sp"),
        P(None, "sp"),
        P(("mem", "sp"), None, None, None),
        P(),
        P(),
        P(),
    )
    return jax.shard_map(
        local,
        mesh=mesh,
        in_specs=placed,
        out_specs=(P("mem", None, "sp"), P(("mem", "sp"), None, None, None)),
        check_vma=False,
    )
```

```python
import functools
import math

import jax
import jax.numpy as jnp
from jax import lax
from jax.experimental import pallas as pl
from jax.experimental.pallas import tpu as pltpu
from jax.sharding import PartitionSpec as P

HD = 128
MTOK = 256
FRAMES_SPAN = 2
CAP = 2
SEL = 8
HALVES = 2
CHUNKS = 2 * HALVES
TOK = MTOK // HALVES
NEG_FILL = -1e30
MESH = pl.DeviceIdType.MESH
VMEM_LIMIT = 58 * 1024 * 1024


def greet(groups, width, g, c):
    barrier = pltpu.get_barrier_semaphore()
    for o in range(1, width):
        pl.semaphore_signal(
            barrier, inc=1, device_id=(g, lax.rem(c + o, width)), device_id_type=MESH
        )
    for o in range(1, groups):
        pl.semaphore_signal(
            barrier, inc=1, device_id=(lax.rem(g + o, groups), c), device_id_type=MESH
        )
    pl.semaphore_wait(barrier, width + groups - 2)


def project_kernel(groups, width, pool, selected, frame_slot, x, wq, wk, wv, mem, qkv, pooled, got, *scratch):
    rows = scratch[:CHUNKS]
    (sendbuf, xg, w3, w_sem, own_sem, mem_send, mem_recv, x_send, x_recv, f_send, f_recv,
     z_send, z_recv, z_own) = scratch[CHUNKS:]
    g = lax.axis_index("mem")
    c = lax.axis_index("sp")
    cols = wq.shape[1]
    block = x.shape[0]
    pairs = width // 2
    me_pair = c // 2
    lane = lax.rem(c, 2)
    sibling = me_pair * 2 + 1 - lane
    lane_rows = pl.ds(pl.multiple_of(lane * block, block), block)
    greet(groups, width, g, c)

    own = []
    sends = []

    def mem_copy(ch, o):
        to = lax.rem(c + o, width)
        return pltpu.make_async_remote_copy(
            src_ref=mem.at[pl.ds(ch * TOK, TOK), pl.ds(pl.multiple_of(to * cols, cols), cols)],
            dst_ref=rows[ch].at[c],
            send_sem=mem_send.at[ch, o],
            recv_sem=mem_recv.at[ch, o],
            device_id=(g, to),
            device_id_type=MESH,
        )

    def x_copy(j):
        to = sibling if j == 0 else lax.rem(c + 2 * j, width)
        return pltpu.make_async_remote_copy(
            src_ref=x,
            dst_ref=xg.at[me_pair, lane_rows],
            send_sem=x_send.at[j],
            recv_sem=x_recv.at[j],
            device_id=(g, to),
            device_id_type=MESH,
        )

    def send_mem(ch):
        copy = pltpu.make_async_copy(
            mem.at[pl.ds(ch * TOK, TOK), pl.ds(pl.multiple_of(c * cols, cols), cols)],
            rows[ch].at[c],
            own_sem.at[ch],
        )
        copy.start()
        own.append(copy)
        for o in range(1, width):
            copy = mem_copy(ch, o)
            copy.start()
            sends.append(copy)

    def send_x(j):
        copy = x_copy(j)
        copy.start()
        sends.append(copy)

    own_x = pltpu.make_async_copy(x, xg.at[me_pair, lane_rows], own_sem.at[CHUNKS])
    w_copies = [
        pltpu.make_async_copy(w, w3.at[i], w_sem.at[i]) for i, w in enumerate((wq, wk, wv))
    ]
    send_mem(0)
    send_x(0)
    own_x.start()
    for copy in w_copies:
        copy.start()

    z_copies = []
    z_local = []

    def picks_of(to):
        found = [jnp.int32(0)] * CAP
        count = jnp.int32(0)
        for j in range(SEL):
            slot = frame_slot[selected[to, j]]
            here = lax.div(slot, width) == g
            column = lax.rem(slot, width)
            found = [jnp.where(here & (count == r), column, found[r]) for r in range(CAP)]
            count = count + jnp.where(here, 1, 0)
        return found

    picks = [picks_of(lax.rem(g + o, groups)) for o in range(groups)]

    def fetch(ch):
        own[ch].wait()
        for o in range(1, width):
            mem_copy(ch, o).wait_recv()
        for o in list(range(1, groups)) + [0]:
            to = lax.rem(g + o, groups)
            for r in range(CAP):
                sendbuf[ch, to, r] = rows[ch][picks[o][r]]
            if o == 0:
                copy = pltpu.make_async_copy(sendbuf.at[ch, g], got.at[ch, g], z_own.at[ch])
                z_local.append(copy)
            else:
                copy = pltpu.make_async_remote_copy(
                    src_ref=sendbuf.at[ch, to],
                    dst_ref=got.at[ch, g],
                    send_sem=z_send.at[ch, o],
                    recv_sem=z_recv.at[ch, o],
                    device_id=(to, c),
                    device_id_type=MESH,
                )
                z_copies.append(copy)
            copy.start()

    small = 2 * block // pool
    row_id = lax.broadcasted_iota(jnp.int32, (small, 2 * block), 0) * pool
    col_id = lax.broadcasted_iota(jnp.int32, (small, 2 * block), 1)
    inside = (col_id >= row_id) & (col_id < row_id + pool)
    averager = jnp.where(inside, 1.0 / pool, 0.0).astype(jnp.bfloat16)
    forwards = []

    def project(j):
        pair = lax.rem(me_pair - j + pairs, pairs)
        x_copy(j).wait_recv()
        if j == 0:
            own_x.wait()
            for copy in w_copies:
                copy.wait()
        else:
            copy = pltpu.make_async_remote_copy(
                src_ref=xg.at[pair, lane_rows],
                dst_ref=xg.at[pair, lane_rows],
                send_sem=f_send.at[j],
                recv_sem=f_recv.at[j],
                device_id=(g, sibling),
                device_id_type=MESH,
            )
            copy.start()
            forwards.append(copy)
            copy.wait_recv()
        out_rows = pl.ds(pl.multiple_of(pair * 2 * block, 2 * block), 2 * block)

        def one(i, carry):
            part = jnp.dot(xg[pair], w3[i], preferred_element_type=jnp.float32)
            qkv[i, out_rows, :] = part.astype(jnp.bfloat16)
            return carry

        lax.fori_loop(0, 3, one, 0)
        small_rows = pl.ds(pl.multiple_of(pair * small, small), small)
        for i in range(2):
            mean = jnp.dot(averager, qkv[i + 1, out_rows, :], preferred_element_type=jnp.float32)
            pooled[i, small_rows, :] = mean.astype(jnp.bfloat16)

    for step in range(max(CHUNKS, pairs + 1)):
        if step < CHUNKS:
            fetch(step)
        if step + 1 < CHUNKS:
            send_mem(step + 1)
        if 1 <= step < pairs:
            send_x(step)
        if step == 0:
            project(0)
        elif 1 <= step - 1 < pairs:
            project(step - 1)

    for copy in sends + forwards:
        copy.wait_send()
    for copy in z_local:
        copy.wait()
    for copy in z_copies:
        copy.wait()


def attend_kernel(groups, width, write_slot, bias, qkv, got, pooled, att, assembled, *scratch):
    arrived = scratch[:CHUNKS]
    wbuf, rbuf, z_send, z_recv, r_send, r_recv, r_own = scratch[CHUNKS:]
    g = lax.axis_index("mem")
    c = lax.axis_index("sp")
    span, cols = att.shape
    heads = cols // HD
    half = got.shape[0] // 2
    greet(groups, width, g, c)
    z_copies = []

    def frame_for(to):
        found = jnp.int32(0)
        for f in range(FRAMES_SPAN):
            found = jnp.where(lax.div(write_slot[g, f], width) == to, f, found)
        return found

    def span_for(to):
        found = jnp.int32(0)
        for span_id in range(groups):
            for f in range(FRAMES_SPAN):
                found = jnp.where(write_slot[span_id, f] == g * width + to, span_id, found)
        return found

    wsel = [frame_for(lax.rem(g + o, groups)) for o in range(groups)]
    rsel = [span_for(lax.rem(c + o, width)) for o in range(width)]

    def send_write(ch):
        for o in list(range(1, groups)) + [0]:
            to = lax.rem(g + o, groups)
            piece = pooled[ch // HALVES, wsel[o], ch % HALVES]
            if o == 0:
                arrived[ch][g] = piece
                continue
            wbuf[ch, to] = piece
            copy = pltpu.make_async_remote_copy(
                src_ref=wbuf.at[ch, to],
                dst_ref=arrived[ch].at[g],
                send_sem=z_send.at[ch, o],
                recv_sem=z_recv.at[ch, o],
                device_id=(to, c),
                device_id_type=MESH,
            )
            copy.start()
            z_copies.append((ch, copy))

    r_copies = []
    r_local = []

    def regroup(ch):
        for at, copy in z_copies:
            if at == ch:
                copy.wait_recv()
        if ch + 2 < CHUNKS:
            send_write(ch + 2)
        for o in list(range(1, width)) + [0]:
            to = lax.rem(c + o, width)
            rbuf[ch, to] = arrived[ch][rsel[o]]
            place = assembled.at[
                pl.ds(ch * TOK, TOK), pl.ds(pl.multiple_of(c * cols, cols), cols)
            ]
            if o == 0:
                copy = pltpu.make_async_copy(rbuf.at[ch, to], place, r_own.at[ch])
                r_local.append(copy)
            else:
                copy = pltpu.make_async_remote_copy(
                    src_ref=rbuf.at[ch, to],
                    dst_ref=place,
                    send_sem=r_send.at[ch, o],
                    recv_sem=r_recv.at[ch, o],
                    device_id=(g, to),
                    device_id_type=MESH,
                )
                r_copies.append(copy)
            copy.start()

    factor = HD ** (-0.5) * math.log2(math.e)
    block = min(256, span)
    nt = (((1,), (1,)), ((), ()))

    def attend(h):
        lanes = slice(h * HD, (h + 1) * HD)

        def one(i, carry):
            rows = pl.ds(pl.multiple_of(i * block, block), block)
            query = qkv[0, rows, lanes]
            own = lax.dot_general(query, qkv[1, :, lanes], nt, preferred_element_type=jnp.float32)
            far = lax.dot_general(
                query, got[0:half, lanes], nt, preferred_element_type=jnp.float32
            )
            if bias is not None:
                far = far + bias[...]
            peak = jnp.maximum(
                jnp.max(own, axis=1, keepdims=True), jnp.max(far, axis=1, keepdims=True)
            )
            own = jnp.exp2((own - peak) * factor)
            far = jnp.exp2((far - peak) * factor)
            totals = jnp.sum(own, axis=1, keepdims=True) + jnp.sum(far, axis=1, keepdims=True)
            mixed = jnp.dot(
                own.astype(jnp.bfloat16), qkv[2, :, lanes], preferred_element_type=jnp.float32
            )
            mixed += jnp.dot(
                far.astype(jnp.bfloat16),
                got[half : 2 * half, lanes],
                preferred_element_type=jnp.float32,
            )
            att[rows, lanes] = (mixed / totals).astype(jnp.bfloat16)
            return carry

        lax.fori_loop(0, span // block, one, 0)

    send_write(0)
    send_write(1)
    for step in range(max(heads, CHUNKS)):
        if step < heads:
            attend(step)
        if step < CHUNKS:
            regroup(step)
    for _, copy in z_copies:
        copy.wait_send()
    for copy in r_local:
        copy.wait()
    for copy in r_copies:
        copy.wait()


def local(span_input, w_query, w_key, w_value, memory_kv, selected, frame_slot, write_slot):
    groups = lax.axis_size("mem")
    width = lax.axis_size("sp")
    g = lax.axis_index("mem")
    c = lax.axis_index("sp")
    depth, cols = w_query.shape
    block = span_input.shape[1]
    span = block * width
    pairs = width // 2
    pool = span // (FRAMES_SPAN * MTOK)
    features = memory_kv.shape[3]

    vmem = pl.BlockSpec(memory_space=pltpu.VMEM)
    smem = pl.BlockSpec(memory_space=pltpu.SMEM)
    anywhere = pl.BlockSpec(memory_space=pl.ANY)
    bf16 = jnp.bfloat16
    dma = pltpu.SemaphoreType.DMA
    qkv, pooled, got = pl.pallas_call(
        functools.partial(project_kernel, groups, width, pool),
        out_shape=(
            jax.ShapeDtypeStruct((3, span, cols), bf16),
            jax.ShapeDtypeStruct((2, FRAMES_SPAN * MTOK, cols), bf16),
            jax.ShapeDtypeStruct((CHUNKS, groups, CAP, TOK, cols), bf16),
        ),
        in_specs=[smem] * 2 + [anywhere] * 5,
        out_specs=(vmem, vmem, anywhere),
        scratch_shapes=[pltpu.VMEM((width, TOK, cols), bf16)] * CHUNKS
        + [
            pltpu.VMEM((CHUNKS, groups, CAP, TOK, cols), bf16),
            pltpu.VMEM((pairs, 2 * block, depth), bf16),
            pltpu.VMEM((3, depth, cols), bf16),
            dma((3,)),
            dma((CHUNKS + 1,)),
            dma((CHUNKS, width)),
            dma((CHUNKS, width)),
            dma((pairs,)),
            dma((pairs,)),
            dma((pairs,)),
            dma((pairs,)),
            dma((CHUNKS, groups)),
            dma((CHUNKS, groups)),
            dma((CHUNKS,)),
        ],
        compiler_params=pltpu.CompilerParams(
            collective_id=0, has_side_effects=True, vmem_limit_bytes=VMEM_LIMIT
        ),
        name="project_and_fetch",
    )(
        selected,
        frame_slot,
        span_input[0],
        w_query,
        w_key,
        w_value,
        memory_kv.reshape(2 * MTOK, features),
    )

    operands = [write_slot]
    specs = [smem]
    kernel = functools.partial(attend_kernel, groups, width)
    if groups * CAP != SEL:
        own_ids = lax.dynamic_index_in_dim(selected, g, 0, keepdims=False)
        own_rows = jnp.take(frame_slot, own_ids, axis=0) // width
        rows_m = jnp.arange(groups, dtype=jnp.int32)
        counts = jnp.sum((own_rows[None, :] == rows_m[:, None]).astype(jnp.int32), axis=1)
        live = jnp.arange(CAP, dtype=jnp.int32)[None, :] < counts[:, None]
        fill = jnp.where(live, 0.0, NEG_FILL).astype(jnp.float32)
        fill = jnp.broadcast_to(fill[None, :, :, None], (HALVES, groups, CAP, TOK))
        operands.append(fill.reshape(1, -1))
        specs.append(vmem)
    else:
        kernel = functools.partial(without_bias, kernel)
    attended, assembled = pl.pallas_call(
        kernel,
        out_shape=(
            jax.ShapeDtypeStruct((span, cols), bf16),
            jax.ShapeDtypeStruct((2 * MTOK, features), bf16),
        ),
        in_specs=specs + [vmem] * 3,
        out_specs=(vmem, anywhere),
        scratch_shapes=[pltpu.VMEM((groups, TOK, cols), bf16)] * CHUNKS
        + [
            pltpu.VMEM((CHUNKS, groups, TOK, cols), bf16),
            pltpu.VMEM((CHUNKS, width, TOK, cols), bf16),
            dma((CHUNKS, groups)),
            dma((CHUNKS, groups)),
            dma((CHUNKS, width)),
            dma((CHUNKS, width)),
            dma((CHUNKS,)),
        ],
        compiler_params=pltpu.CompilerParams(
            collective_id=1, has_side_effects=True, vmem_limit_bytes=VMEM_LIMIT
        ),
        name="attend_and_write",
    )(
        *operands,
        qkv,
        got.reshape(-1, cols),
        pooled.reshape(2, FRAMES_SPAN, HALVES, TOK, cols),
    )
    written = jnp.any(write_slot == g * width + c)
    new_memory = jnp.where(written, assembled.reshape(memory_kv.shape), memory_kv)
    return (attended[None], new_memory)


def without_bias(kernel, write_slot, *rest):
    kernel(write_slot, None, *rest)


def solution(mesh):
    placed = (
        P("mem", "sp", None),
        P(None, "sp"),
        P(None, "sp"),
        P(None, "sp"),
        P(("mem", "sp"), None, None, None),
        P(),
        P(),
        P(),
    )
    return jax.shard_map(
        local,
        mesh=mesh,
        in_specs=placed,
        out_specs=(P("mem", None, "sp"), P(("mem", "sp"), None, None, None)),
        check_vma=False,
    )
```
